512 devices in a mesh: ctx: 128 (over y, z, core), ch: 4 (over x).
Axes of the slice: x: 4, y: 8, z: 8, core: 2. Of those that a mesh axis runs over, the one named last changes fastest.
Arguments:
- query_act: bfloat16 [16384, 4096], P('ctx', 'ch'), may hold values from -6 to 6
- key_act: bfloat16 [16384, 4096], P('ctx', 'ch'), may hold values from -6 to 6
- value_act: bfloat16 [16384, 4096], P('ctx', 'ch'), may hold values from -6 to 6
- short_filter: float32 [128, 4096], P(None, 'ch'), may hold values from -0.5 to 0.5
- long_filter: float32 [16384, 4096], P('ctx', 'ch'), may hold values from -2 to 2
- out_weight: bfloat16 [4096, 4096], P('ch', 'ctx'), may hold values from -0.09375 to 0.09375
Outputs:
- mixed: bfloat16 [16384, 4096], P('ctx', 'ch')
The draws below stay inside these ranges and needn't reach their ends.
All inputs are finite; a program needn't handle non-finite values.
Results may differ from the reference program's by a relative error of at most 0.02.
Values may be sent and summed in bfloat16 or wider, within the bound.
A program may use at most 128 MiB of HBM per device.

```python
import math
import jax
import jax.numpy as jnp
from jax import lax

D = 4096
TAPS = 128
TOKENS = 16384


def draw_long_filter(key, part):
    lags = jnp.arange(TOKENS, dtype=jnp.float32)[:, None]
    spread = jax.random.uniform(jax.random.fold_in(key, 11), (1, D), jnp.float32)
    low_end = math.log(16.0)
    high_end = math.log(TOKENS * 4.0)
    lifetime = jnp.exp(low_end + (high_end - low_end) * spread)
    rough = jnp.clip(jax.random.normal(jax.random.fold_in(key, 12), (TOKENS, D), jnp.float32), -4.0, 4.0)
    return rough * jnp.sqrt(2.0 / lifetime) * jnp.exp(-lags / lifetime)


def levels(stream_key, dims, shards, smallest, high):
    def one(dim, parts):
        steps = jax.random.uniform(jax.random.fold_in(jax.random.fold_in(stream_key, 6), dim), (parts,), jnp.float32, smallest / len(shards), high / len(shards))
        return jnp.repeat(jnp.exp(steps), dims[dim] // parts).reshape((-1,) + (1,) * (len(dims) - dim - 1))

    gain = one(*shards[0])
    for cut in shards[1:]:
        gain = gain * one(*cut)
    return gain


def scatter_about(stream_key, extent, deviation, limit, cuts=(), held_as=jnp.bfloat16):
    values = jax.random.normal(stream_key, extent, jnp.float32) * deviation
    if len(cuts) > 0:
        values = levels(stream_key, extent, cuts, -0.22, 0.18) * values
    return jnp.clip(values, min=-limit, max=limit).astype(held_as)


def setup_inputs(seed: int = 0) -> dict:
    splits = jax.random.split(jax.random.key(seed), 7)
    query_act = scatter_about(splits[0], (TOKENS, D), 1.0, 6.0, ((0, 128), (1, 4)))
    key_act = scatter_about(splits[1], (TOKENS, D), 1.0, 6.0, ((0, 128), (1, 4)))
    value_act = scatter_about(splits[2], (TOKENS, D), 1.0, 6.0, ((0, 128), (1, 4)))
    short_filter = scatter_about(splits[3], (TAPS, D), TAPS ** -0.5, 0.5, ((1, 4),), jnp.float32)
    long_filter = draw_long_filter(jax.random.fold_in(splits[6], 71), 0)
    out_weight = scatter_about(splits[5], (D, D), D ** -0.5, 0.09375, ((0, 4), (1, 128)))
    return dict(query_act=query_act, key_act=key_act, value_act=value_act, short_filter=short_filter, long_filter=long_filter, out_weight=out_weight)


def short_conv(product, filter_block):
    taps_count = filter_block.shape[0]
    total_rows = product.shape[0]
    padded = jnp.pad(product, ((taps_count - 1, 0), (0, 0)))

    def one_tap(tap_index, accum):
        start_row = (taps_count - 1 - tap_index).astype(jnp.int32)
        window = lax.dynamic_slice_in_dim(padded, start_row, total_rows, 0)
        weights = lax.dynamic_slice_in_dim(filter_block, tap_index.astype(jnp.int32), 1, 0)
        return accum + weights * window

    return lax.fori_loop(0, taps_count, one_tap, jnp.zeros(product.shape, jnp.float32))


def long_conv(operands):
    signal, coeffs = operands
    total_rows = signal.shape[0]
    spectrum = jnp.fft.rfft(signal, n=2 * total_rows, axis=0) * jnp.fft.rfft(coeffs, n=2 * total_rows, axis=0)
    return jnp.fft.irfft(spectrum, n=2 * total_rows, axis=0)[:total_rows]


def reference(query_act, key_act, value_act, short_filter, long_filter, out_weight):
    full_width = query_act.shape[1]
    block_width = min(256, full_width)
    block_count = full_width // block_width

    def to_blocks(array):
        return array.reshape(array.shape[0], block_count, block_width).transpose(1, 0, 2)

    def from_blocks(array):
        return array.transpose(1, 0, 2).reshape(array.shape[1], full_width)

    product = key_act.astype(jnp.float32) * value_act.astype(jnp.float32)
    short_mix = from_blocks(lax.map(lambda operands: short_conv(operands[0], operands[1]), (to_blocks(product), to_blocks(short_filter))))
    gated_mix = (query_act.astype(jnp.float32) * short_mix).astype(jnp.bfloat16)
    long_mix = from_blocks(lax.map(long_conv, (to_blocks(gated_mix.astype(jnp.float32)), to_blocks(long_filter)))).astype(jnp.bfloat16)
    hidden = (value_act.astype(jnp.float32) * long_mix.astype(jnp.float32)).astype(jnp.bfloat16)
    return jnp.dot(hidden, out_weight, preferred_element_type=jnp.float32).astype(jnp.bfloat16)
```

```python
import math

import jax
import jax.numpy as jnp
import numpy as np
from jax import lax
from jax.experimental import pallas as pl
from jax.experimental.pallas import tpu as pltpu
from jax.sharding import PartitionSpec as P

NX, NY, NZ = 4, 8, 8
CHIPS = NY * NZ
TOK = 128
WIDTH = 1024
OWN = 8
MESH = pl.DeviceIdType.MESH
F32, BF16 = jnp.float32, jnp.bfloat16


def split_table(table):
    high = table.astype(jnp.bfloat16)
    low = (table - high.astype(np.float64)).astype(jnp.bfloat16)
    return high, low


def make_tables():
    blocks = 2 * CHIPS
    half_odd = np.arange(blocks) + 0.5
    index = np.arange(blocks)
    angle = 2 * math.pi * half_odd[:, None] * index[None, :] / (2 * blocks)
    first = np.concatenate([np.cos(angle), -np.sin(angle)], 0)
    fold = split_table(first)
    first_cat = np.concatenate(fold, 1)
    last = split_table(first.T * (2.0 / (2 * blocks * TOK)))
    inner = 2 * math.pi * (np.arange(TOK)[:, None] * np.arange(TOK)[None, :] % TOK) / TOK
    cosine, minus_sine = np.cos(inner), -np.sin(inner)
    second = np.block([[cosine, minus_sine], [-minus_sine, cosine]])
    second_split = split_table(second)
    third_split = split_table(second.T)
    turn = 2 * math.pi * half_odd[:, None] * np.arange(TOK)[None, :] / (2 * blocks * TOK)
    return (
        first_cat,
        np.stack(last),
        np.stack(second_split),
        np.stack(third_split),
        np.stack([np.cos(turn), -np.sin(turn)]).astype(np.float32),
    )


def dot(a, b):
    return jnp.dot(a, b, preferred_element_type=F32)


def halves(value):
    high = value.astype(BF16)
    return high, (value - high.astype(F32)).astype(BF16)


def kernel(
    q_ref, k_ref, v_ref, sf_ref, lf_ref, wt_ref,
    first_ref, last_ref, second_ref, third_ref, turn_ref,
    out_ref,
    tf, tp, tq, ys, taps_t,
    exf_out, exf_in, exp_out, exp_in, exr_out, exr_in,
    send_f, recv_f, send_pq, recv_pq, send_r, recv_r,
    toep, spectrum, wall, hidden,
    hop_out, hop_in, right_out, left_out, from_left, from_right, part_r, part_l,
    ex_send, ex_recv, a_send, a_recv, w1_send, w1_recv, w2_send, w2_recv, wp_send, wp_recv,
    x_send, x_recv,
):
    me = lax.axis_index("ctx")
    x = lax.axis_index("ch")
    m, s = me // 2, me % 2
    o = 1 - s
    y, z = m // NZ, m % NZ
    partner = 2 * m + o
    x_right, x_left = (x + 1) % NX, (x + NX - 1) % NX

    def plane(chip):
        return {"ctx": 2 * chip + s}

    barrier = pltpu.get_barrier_semaphore()

    def greet(i, carry):
        pl.semaphore_signal(barrier, inc=1, device_id=plane((m + i) % CHIPS), device_id_type=MESH)
        return carry

    lax.fori_loop(1, CHIPS, greet, 0)
    pl.semaphore_signal(barrier, inc=1, device_id={"ctx": partner}, device_id_type=MESH)
    pl.semaphore_signal(barrier, inc=1, device_id={"ch": x_right}, device_id_type=MESH)
    pl.semaphore_signal(barrier, inc=1, device_id={"ch": x_left}, device_id_type=MESH)

    def remote(src, dst, send, recv, device):
        return pltpu.make_async_remote_copy(
            src_ref=src, dst_ref=dst, send_sem=send, recv_sem=recv,
            device_id=device, device_id_type=MESH,
        )

    def arrived(ref, sem):
        pltpu.make_async_copy(ref, ref, sem).wait()

    for j in range(WIDTH // 128):
        lanes = slice(128 * j, 128 * j + 128)
        rows = slice(8 * j, 8 * j + 8)
        tf[rows] = lf_ref[:, lanes].T.reshape(8, 2, OWN, TOK)
    exf_out[...] = tf[:, o].reshape(CHIPS * OWN, TOK).astype(BF16)
    for j in range(WIDTH // 128):
        lanes = slice(128 * j, 128 * j + 128)
        rows = slice(8 * j, 8 * j + 8)
        tp[rows] = (k_ref[:, lanes].astype(F32) * v_ref[:, lanes].astype(F32)).T.reshape(8, 2, OWN, TOK)
        tq[rows] = q_ref[:, lanes].astype(F32).T.reshape(8, 2, OWN, TOK)
    exp_out[0] = tp[:, o].reshape(CHIPS * OWN, TOK).astype(BF16)
    exp_out[1] = tq[:, o].reshape(CHIPS * OWN, TOK).astype(BF16)

    pl.semaphore_wait(barrier, CHIPS + 2)

    swap_f = remote(exf_out, exf_in, ex_send.at[0], ex_recv.at[0], {"ctx": partner})
    swap_p = remote(exp_out, exp_in, ex_send.at[1], ex_recv.at[1], {"ctx": partner})
    swap_f.start()
    swap_p.start()

    swap_f.wait()
    tf[:, o] = exf_in[...].astype(F32).reshape(CHIPS, OWN, TOK)
    send_f[...] = tf[...].reshape(CHIPS, 2 * OWN, TOK).astype(BF16)

    def spread(src, dst, which):
        pltpu.make_async_copy(src.at[m], dst.at[m], a_recv.at[which]).start()

        def one(i, carry):
            chip = (m + i) % CHIPS
            remote(src.at[chip], dst.at[m], a_send.at[which], a_recv.at[which], plane(chip)).start()
            return carry

        lax.fori_loop(1, CHIPS, one, 0)

    def gathered(src, dst, which):
        arrived(dst, a_recv.at[which])
        arrived(src.at[pl.ds(0, CHIPS - 1)], a_send.at[which])

    spread(send_f, recv_f, 0)
    swap_p.wait()
    tp[:, o] = exp_in[0].astype(F32).reshape(CHIPS, OWN, TOK)
    tq[:, o] = exp_in[1].astype(F32).reshape(CHIPS, OWN, TOK)
    send_pq[:, : 2 * OWN] = tp[...].reshape(CHIPS, 2 * OWN, TOK).astype(BF16)
    send_pq[:, 2 * OWN :] = tq[...].reshape(CHIPS, 2 * OWN, TOK).astype(BF16)
    spread(send_pq, recv_pq, 1)

    for h in range(2):
        pltpu.make_async_copy(wt_ref.at[pl.ds(16 * h, 16)], wall.at[y, z, s, h], w1_recv.at[h]).start()
    for i in range(1, 8):
        remote(
            wt_ref.at[pl.ds(0, 16)], wall.at[y, z, s, 0], w1_send, w1_recv.at[0],
            plane(y * NZ + (z + i) % NZ),
        ).start()
        remote(
            wt_ref.at[pl.ds(16, 16)], wall.at[y, z, s, 1], w1_send, w1_recv.at[1],
            plane((y + i) % NY * NZ + z),
        ).start()

    y_right, y_left = (y + 1) % NY, (y + NY - 1) % NY
    z_right, z_left = (z + 1) % NZ, (z + NZ - 1) % NZ

    def chunk(h, offset, part=None):
        span = slice(None) if part is None else pl.ds(4 * part, 4)
        if h == 0:
            return wall.at[(y + offset + NY) % NY, span, s, 0]
        return wall.at[span, (z + offset + NZ) % NZ, s, 1]

    def toward(h, right):
        if h == 0:
            return plane((y_right if right else y_left) * NZ + z)
        return plane(y * NZ + (z_right if right else z_left))

    def share(ref):
        remote(ref, ref, wp_send, wp_recv, {"ctx": partner}).start()

    def weight_step(j):
        for h in range(2):
            if j == 0:
                arrived(chunk(h, 0), w1_recv.at[h])
                share(chunk(h, 0))
            elif j < 4:
                arrived(chunk(h, -j), w2_recv.at[h, 0, j - 1])
                arrived(chunk(h, j), w2_recv.at[h, 1, j - 1])
            else:
                arrived(chunk(h, 4, 0), w2_recv.at[h, 0, 3])
                arrived(chunk(h, 4, 1), w2_recv.at[h, 1, 3])
                share(chunk(h, 4))
            if j < 4:
                part_right, part_left = (0, 1) if j == 3 else (None, None)
                right, left = chunk(h, -j, part_right), chunk(h, j, part_left)
                remote(right, right, w2_send, w2_recv.at[h, 0, j], toward(h, True)).start()
                remote(left, left, w2_send, w2_recv.at[h, 1, j], toward(h, False)).start()
            if 0 < j < 4:
                share(chunk(h, -j))
                share(chunk(h, j))

    taps_t[...] = sf_ref[:, pl.ds(pl.multiple_of(me // 16 * 128, 128), 128)].T

    def forward(signal):
        stage = dot(first_ref[...], jnp.concatenate([signal, signal], 0))
        real, imag = stage[:TOK], stage[TOK:]
        turn_real, turn_imag = turn_ref[0], turn_ref[1]
        turned = jnp.concatenate(
            [real * turn_real - imag * turn_imag, real * turn_imag + imag * turn_real], 1
        )
        high, low = halves(turned)
        return dot(high, second_ref[0]) + dot(low, second_ref[0]) + dot(high, second_ref[1])

    def toeplitz(c, carry):
        row = taps_t[pl.ds(me % 16 * OWN + c, 1), :]
        base = jnp.concatenate([row, jnp.zeros_like(row)], 1)
        square = pltpu.roll(jnp.broadcast_to(base, (TOK, 2 * TOK)), 0, 1, stride=1, stride_axis=0)
        high, low = halves(square)
        toep[c] = jnp.concatenate([high, low], 0)
        return carry

    lax.fori_loop(0, OWN, toeplitz, 0)

    gathered(send_f, recv_f, 0)
    flat_f = tf.reshape(CHIPS * 2 * OWN, TOK)
    flat_p = tp.reshape(CHIPS * 2 * OWN, TOK)
    flat_q = tq.reshape(CHIPS * 2 * OWN, TOK)
    flat_y = ys.reshape(CHIPS * 2 * OWN, TOK)
    flat_f[...] = recv_f[...].astype(F32).reshape(CHIPS * 2 * OWN, TOK)

    def filter_spectrum(c, carry):
        spectrum[c] = forward(flat_f[pl.ds(c, TOK, stride=OWN), :].astype(BF16))
        return carry

    lax.fori_loop(0, OWN, filter_spectrum, 0)
    weight_step(0)

    gathered(send_pq, recv_pq, 1)
    flat_p[...] = recv_pq[:, : 2 * OWN].astype(F32).reshape(CHIPS * 2 * OWN, TOK)
    flat_q[...] = recv_pq[:, 2 * OWN :].astype(F32).reshape(CHIPS * 2 * OWN, TOK)

    def convolve(c, carry):
        product = flat_p[pl.ds(c, TOK, stride=OWN), :].astype(BF16)
        query = flat_q[pl.ds(c, TOK, stride=OWN), :]
        spread_out = dot(jnp.concatenate([product, product], 1), toep[c])
        spill = pltpu.roll(spread_out[:, TOK:], 1, 0)
        rows = lax.broadcasted_iota(jnp.int32, (TOK, TOK), 0)
        short_mix = spread_out[:, :TOK] + jnp.where(rows == 0, 0.0, spill)
        gated = (query * short_mix).astype(BF16)
        signal = forward(gated)
        other = spectrum[c]
        real, imag = signal[:, :TOK], signal[:, TOK:]
        other_real, other_imag = other[:, :TOK], other[:, TOK:]
        joint = jnp.concatenate(
            [real * other_real - imag * other_imag, real * other_imag + imag * other_real], 1
        )
        high, low = halves(joint)
        mixed = dot(high, third_ref[0]) + dot(low, third_ref[0]) + dot(high, third_ref[1])
        real, imag = mixed[:, :TOK], mixed[:, TOK:]
        turn_real, turn_imag = turn_ref[0], turn_ref[1]
        back = jnp.concatenate(
            [real * turn_real + imag * turn_imag, imag * turn_real - real * turn_imag], 0
        )
        high, low = halves(back)
        flat_y[pl.ds(c, TOK, stride=OWN), :] = (
            dot(last_ref[0], high) + dot(last_ref[0], low) + dot(last_ref[1], high)
        )
        return carry

    lax.fori_loop(0, OWN // 2, convolve, 0)
    weight_step(1)
    lax.fori_loop(OWN // 2, OWN, convolve, 0)

    exr_out[...] = ys[:, o].reshape(CHIPS * OWN, TOK).astype(BF16)
    swap_r = remote(exr_out, exr_in, ex_send.at[2], ex_recv.at[2], {"ctx": partner})
    swap_r.start()
    swap_r.wait()
    ys[:, o] = exr_in[...].astype(F32).reshape(CHIPS, OWN, TOK)
    send_r[...] = ys[...].reshape(CHIPS, 2 * OWN, TOK).astype(BF16)
    spread(send_r, recv_r, 2)
    weight_step(2)
    gathered(send_r, recv_r, 2)

    for j in range(WIDTH // 128):
        lanes = slice(128 * j, 128 * j + 128)
        block = recv_r[8 * j : 8 * j + 8].astype(F32).reshape(128, TOK).T
        hidden[:, lanes] = (v_ref[:, lanes].astype(F32) * block).astype(BF16)
    weight_step(3)
    weight_step(4)
    arrived(wall.at[:, :, o], wp_recv)

    def project(block, t):
        rows = wall[2 * block + t // 2, pl.ds(4 * (t % 2), 4)].reshape(256, WIDTH)
        return lax.dot_general(
            hidden[...], rows, (((1,), (1,)), ((), ())), preferred_element_type=F32
        )

    for t in range(4):
        hop_out[t // 2, :, 256 * (t % 2) : 256 * (t % 2) + 256] = project((x + 2) % NX, t).astype(BF16)
    hop_a = remote(hop_out.at[0], hop_in.at[0], x_send.at[0], x_recv.at[0], {"ch": x_right})
    hop_b = remote(hop_out.at[1], hop_in.at[1], x_send.at[1], x_recv.at[1], {"ch": x_left})
    hop_a.start()
    hop_b.start()
    for t in range(4):
        part_r[t // 2, :, 256 * (t % 2) : 256 * (t % 2) + 256] = project(x_right, t)
        part_l[t // 2, :, 256 * (t % 2) : 256 * (t % 2) + 256] = project(x_left, t)
    right_out[1] = part_r[1].astype(BF16)
    left_out[0] = part_l[0].astype(BF16)
    hop_a.wait()
    right_out[0] = (part_r[0] + hop_in[0].astype(F32)).astype(BF16)
    hop_b.wait()
    left_out[1] = (part_l[1] + hop_in[1].astype(F32)).astype(BF16)
    go_right = remote(right_out, from_left, x_send.at[2], x_recv.at[2], {"ch": x_right})
    go_left = remote(left_out, from_right, x_send.at[3], x_recv.at[3], {"ch": x_left})
    go_right.start()
    go_left.start()
    for t in range(4):
        part_r[t // 2, :, 256 * (t % 2) : 256 * (t % 2) + 256] = project(x, t)
    go_right.wait()
    go_left.wait()
    for h in range(2):
        total = part_r[h] + from_left[h].astype(F32) + from_right[h].astype(F32)
        out_ref[:, 512 * h : 512 * h + 512] = total.astype(BF16)

    arrived(wall.at[0, pl.ds(0, 7), s], w1_send)
    arrived(wall.at[pl.ds(0, 7), :, s], w2_send)
    arrived(wall.at[:, :, s], wp_send)


def local(query_act, key_act, value_act, short_filter, long_filter, out_weight):
    tables = make_tables()
    vmem = pl.BlockSpec(memory_space=pltpu.VMEM)
    rows = CHIPS * OWN
    block_f32 = pltpu.VMEM((CHIPS, 2, OWN, TOK), F32)
    half_bf16 = pltpu.VMEM((rows, TOK), BF16)
    pair_bf16 = pltpu.VMEM((2, rows, TOK), BF16)
    tiles = pltpu.VMEM((CHIPS, 2 * OWN, TOK), BF16)
    wide_tiles = pltpu.VMEM((CHIPS, 4 * OWN, TOK), BF16)
    share_bf16 = pltpu.VMEM((2, TOK, WIDTH // 2), BF16)
    share_f32 = pltpu.VMEM((2, TOK, WIDTH // 2), F32)
    dma = pltpu.SemaphoreType.DMA
    return pl.pallas_call(
        kernel,
        out_shape=jax.ShapeDtypeStruct((TOK, WIDTH), BF16),
        in_specs=[vmem] * (6 + len(tables)),
        out_specs=vmem,
        scratch_shapes=[
            block_f32, block_f32, block_f32, block_f32, pltpu.VMEM((TOK, 128), F32),
            half_bf16, half_bf16, pair_bf16, pair_bf16, half_bf16, half_bf16,
            tiles, tiles, wide_tiles, wide_tiles, tiles, tiles,
            pltpu.VMEM((OWN, 2 * TOK, 2 * TOK), BF16),
            pltpu.VMEM((OWN, TOK, 2 * TOK), F32),
            pltpu.VMEM((NY, NZ, 2, 2, 16, WIDTH), BF16),
            pltpu.VMEM((TOK, WIDTH), BF16),
            share_bf16, share_bf16, share_bf16, share_bf16, share_bf16, share_bf16,
            share_f32, share_f32,
            dma((3,)), dma((3,)), dma((3,)), dma((3,)), dma, dma((2,)), dma, dma((2, 2, 4)), dma, dma,
            dma((4,)), dma((4,)),
        ],
        compiler_params=pltpu.CompilerParams(
            collective_id=0, has_side_effects=True, vmem_limit_bytes=48 * 1024 * 1024
        ),
    )(query_act, key_act, value_act, short_filter, long_filter, out_weight.T, *tables)


def solution(mesh):
    placed = (
        P("ctx", "ch"),
        P("ctx", "ch"),
        P("ctx", "ch"),
        P(None, "ch"),
        P("ctx", "ch"),
        P("ch", "ctx"),
    )
    return jax.shard_map(
        local, mesh=mesh, in_specs=placed, out_specs=P("ctx", "ch"), check_vma=False
    )
```

```python
import math

import jax
import jax.numpy as jnp
import numpy as np
from jax import lax
from jax.experimental import pallas as pl
from jax.experimental.pallas import tpu as pltpu
from jax.sharding import PartitionSpec as P

NX, NY, NZ = 4, 8, 8
CHIPS = NY * NZ
TOK = 128
WIDTH = 1024
OWN = 8
MESH = pl.DeviceIdType.MESH
F32, BF16 = jnp.float32, jnp.bfloat16


def split_table(table):
    high = table.astype(jnp.bfloat16)
    low = (table - high.astype(np.float64)).astype(jnp.bfloat16)
    return high, low


def make_tables():
    blocks = 2 * CHIPS
    half_odd = np.arange(blocks) + 0.5
    index = np.arange(blocks)
    angle = 2 * math.pi * half_odd[:, None] * index[None, :] / (2 * blocks)
    first = np.concatenate([np.cos(angle), -np.sin(angle)], 0)
    fold = split_table(first)
    first_cat = np.concatenate(fold, 1)
    last = split_table(first.T * (2.0 / (2 * blocks * TOK)))
    inner = 2 * math.pi * (np.arange(TOK)[:, None] * np.arange(TOK)[None, :] % TOK) / TOK
    cosine, minus_sine = np.cos(inner), -np.sin(inner)
    second = np.block([[cosine, minus_sine], [-minus_sine, cosine]])
    second_split = split_table(second)
    third_split = split_table(second.T)
    turn = 2 * math.pi * half_odd[:, None] * np.arange(TOK)[None, :] / (2 * blocks * TOK)
    order = np.zeros((512, 512))
    column = np.arange(512)
    order[column // 16 % 2 * 256 + column // 32 * 16 + column % 16, column] = 1.0
    return (
        first_cat,
        np.stack(last),
        np.stack(second_split),
        np.stack(third_split),
        np.stack([np.cos(turn), -np.sin(turn)]).astype(np.float32),
        order.astype(jnp.bfloat16),
    )


def dot(a, b):
    return jnp.dot(a, b, preferred_element_type=F32)


def halves(value):
    high = value.astype(BF16)
    return high, (value - high.astype(F32)).astype(BF16)


def kernel(
    q_hbm, k_hbm, v_hbm, sf_hbm, lf_hbm, wt_ref,
    first_hbm, last_hbm, second_hbm, third_hbm, turn_hbm, order_hbm,
    out_ref,
    q_ref, k_ref, v_ref, sf_ref, lf_ref,
    first_ref, last_ref, second_ref, third_ref, turn_ref, order_ref, load_sems,
    ext, short, halo_out, halo_in,
    tf, tg, ys,
    exf_out, exf_in, exg_out, exg_in, exr_out, exr_in,
    send_f, recv_f, send_g, recv_g, send_r, recv_r,
    spectrum, wall, hidden,
    hop_out, hop_in, right_out, left_out, from_left, from_right, part_r, part_l,
    ex_send, ex_recv, a_send, a_recv, w1_send, w1_recv, w2_send, w2_recv, wp_send, wp_recv,
    x_send, x_recv,
):
    me = lax.axis_index("ctx")
    x = lax.axis_index("ch")
    m, s = me // 2, me % 2
    o = 1 - s
    y, z = m // NZ, m % NZ
    partner = 2 * m + o
    after = (me + 1) % (2 * CHIPS)
    x_right, x_left = (x + 1) % NX, (x + NX - 1) % NX

    def plane(chip):
        return {"ctx": 2 * chip + s}

    loads = [
        pltpu.make_async_copy(src, dst, load_sems.at[i])
        for i, (src, dst) in enumerate([
            (k_hbm, k_ref), (v_hbm, v_ref), (lf_hbm, lf_ref), (sf_hbm, sf_ref), (q_hbm, q_ref),
            (first_hbm, first_ref), (second_hbm, second_ref), (turn_hbm, turn_ref),
            (third_hbm, third_ref), (last_hbm, last_ref), (order_hbm, order_ref),
        ])
    ]
    for load in loads:
        load.start()

    barrier = pltpu.get_barrier_semaphore()

    def greet(i, carry):
        pl.semaphore_signal(barrier, inc=1, device_id=plane((m + i) % CHIPS), device_id_type=MESH)
        return carry

    lax.fori_loop(1, CHIPS, greet, 0)
    other_chip = (m + 2 * s - 1 + CHIPS) % CHIPS
    for device in (
        {"ctx": partner}, {"ctx": 2 * other_chip + o}, {"ch": x_right}, {"ch": x_left},
    ):
        pl.semaphore_signal(barrier, inc=1, device_id=device, device_id_type=MESH)

    def remote(src, dst, send, recv, device):
        return pltpu.make_async_remote_copy(
            src_ref=src, dst_ref=dst, send_sem=send, recv_sem=recv,
            device_id=device, device_id_type=MESH,
        )

    def arrived(ref, sem):
        pltpu.make_async_copy(ref, ref, sem).wait()

    y_right, y_left = (y + 1) % NY, (y + NY - 1) % NY
    z_right, z_left = (z + 1) % NZ, (z + NZ - 1) % NZ

    def half_lanes(h):
        return pl.ds(512 * h, 512)

    def chunk(h, offset, r, part=None):
        span = slice(None) if part is None else pl.ds(4 * part, 4)
        if h == 0:
            return wall.at[(y + offset + NY) % NY, span, s, r, :, half_lanes(h)]
        return wall.at[span, (z + offset + NZ) % NZ, s, r, :, half_lanes(h)]

    def toward(h, right):
        if h == 0:
            return plane((y_right if right else y_left) * NZ + z)
        return plane(y * NZ + (z_right if right else z_left))

    def share(ref, r):
        remote(ref, ref, wp_send, wp_recv.at[r], {"ctx": partner}).start()

    def weight_start():
        for r in range(2):
            for h in range(2):
                src = wt_ref.at[pl.ds(16 * r, 16), half_lanes(h)]
                dst = wall.at[y, z, s, r, :, half_lanes(h)]
                pltpu.make_async_copy(src, dst, w1_recv.at[r, h]).start()
                for i in range(1, 8):
                    chip = y * NZ + (z + i) % NZ if h == 0 else (y + i) % NY * NZ + z
                    remote(src, dst, w1_send, w1_recv.at[r, h], plane(chip)).start()

    def weight_step(j, r):
        for h in range(2):
            if j == 0:
                arrived(chunk(h, 0, r), w1_recv.at[r, h])
                share(chunk(h, 0, r), r)
            elif j < 4:
                arrived(chunk(h, -j, r), w2_recv.at[h, 0, j - 1, r])
                arrived(chunk(h, j, r), w2_recv.at[h, 1, j - 1, r])
            else:
                arrived(chunk(h, 4, r, 0), w2_recv.at[h, 0, 3, r])
                arrived(chunk(h, 4, r, 1), w2_recv.at[h, 1, 3, r])
                share(chunk(h, 4, r), r)
            if j < 4:
                for side in range(2):
                    moved = chunk(h, j if side else -j, r, side if j == 3 else None)
                    remote(
                        moved, moved, w2_send, w2_recv.at[h, side, j, r], toward(h, side == 0)
                    ).start()
            if 0 < j < 4:
                share(chunk(h, -j, r), r)
                share(chunk(h, j, r), r)

    loads[0].wait()
    loads[1].wait()
    for j in range(WIDTH // 128):
        lanes = slice(128 * j, 128 * j + 128)
        product = k_ref[:, lanes].astype(F32) * v_ref[:, lanes].astype(F32)
        ext[j, TOK:] = product
        halo_out[j] = product.astype(BF16)

    loads[2].wait()
    for j in range(WIDTH // 128):
        lanes = slice(128 * j, 128 * j + 128)
        tf[8 * j : 8 * j + 8] = lf_ref[:, lanes].T.reshape(8, 2, OWN, TOK)
    exf_out[...] = tf[:, o].reshape(CHIPS * OWN, TOK).astype(BF16)
    loads[3].wait()

    def short_part(j, prior):
        lanes = pl.ds(pl.multiple_of(j * 128, 128), 128)
        if prior:
            accum = [short[j, 8 * i : 8 * i + 8] for i in range(16)]
        else:
            accum = [jnp.zeros((8, 128), F32) for i in range(16)]
        for r in range(8):
            ranks = range(1, 17) if prior else range(17, 32)
            windows = {u: ext[j, 8 * u - r : 8 * u - r + 8] for u in ranks}
            for q in range(16):
                taps = jnp.broadcast_to(sf_ref[8 * q + r : 8 * q + r + 1, lanes], (8, 128))
                for i in range(0, q + 1) if prior else range(q + 1, 16):
                    accum[i] = accum[i] + taps * windows[i - q + 16]
        for i in range(16):
            short[j, 8 * i : 8 * i + 8] = accum[i]

    def short_own(j, carry):
        short_part(j, False)
        return carry

    def short_prior(j, carry):
        short_part(j, True)
        return carry

    lax.fori_loop(0, WIDTH // 128, short_own, 0)

    pl.semaphore_wait(barrier, CHIPS + 3)

    halo = remote(halo_out, halo_in, ex_send.at[1], ex_recv.at[1], {"ctx": after})
    halo.start()
    weight_start()

    swap_f = remote(exf_out, exf_in, ex_send.at[0], ex_recv.at[0], {"ctx": partner})
    swap_f.start()

    def spread(src, dst, which):
        pltpu.make_async_copy(src.at[m], dst.at[m], a_recv.at[which]).start()

        def one(i, carry):
            chip = (m + i) % CHIPS
            remote(src.at[chip], dst.at[m], a_send.at[which], a_recv.at[which], plane(chip)).start()
            return carry

        lax.fori_loop(1, CHIPS, one, 0)

    def gathered(src, dst, which):
        arrived(dst, a_recv.at[which])
        arrived(src.at[pl.ds(0, CHIPS - 1)], a_send.at[which])

    swap_f.wait()
    tf[:, o] = exf_in[...].astype(F32).reshape(CHIPS, OWN, TOK)
    send_f[...] = tf[...].reshape(CHIPS, 2 * OWN, TOK).astype(BF16)
    spread(send_f, recv_f, 0)
    halo.wait()
    loads[4].wait()
    first_device = me == 0
    for j in range(WIDTH // 128):
        ext[j, :TOK] = jnp.where(first_device, 0.0, halo_in[j].astype(F32))
    lax.fori_loop(0, WIDTH // 128, short_prior, 0)
    for j in range(WIDTH // 128):
        lanes = slice(128 * j, 128 * j + 128)
        tg[8 * j : 8 * j + 8] = (q_ref[:, lanes].astype(F32) * short[j]).T.reshape(8, 2, OWN, TOK)
    exg_out[...] = tg[:, o].reshape(CHIPS * OWN, TOK).astype(BF16)
    swap_g = remote(exg_out, exg_in, ex_send.at[3], ex_recv.at[3], {"ctx": partner})
    swap_g.start()
    weight_step(0, 0)
    swap_g.wait()
    tg[:, o] = exg_in[...].astype(F32).reshape(CHIPS, OWN, TOK)
    send_g[...] = tg[...].reshape(CHIPS, 2 * OWN, TOK).astype(BF16)
    spread(send_g, recv_g, 1)
    weight_step(0, 1)
    for load in loads[5:]:
        load.wait()
    flat_f = tf.reshape(CHIPS * 2 * OWN, TOK)
    flat_g = tg.reshape(CHIPS * 2 * OWN, TOK)
    flat_y = ys.reshape(CHIPS * 2 * OWN, TOK)

    def tile(value, c):
        return value[:, TOK * c : TOK * c + TOK]

    def times(value, table):
        high, low = halves(value)
        return dot(high, table[0]) + dot(low, table[0]) + dot(high, table[1])

    def forward(flat, base):
        signal = jnp.concatenate(
            [flat[pl.ds(base + c, TOK, stride=OWN), :].astype(BF16) for c in range(4)], 1
        )
        stage = dot(first_ref[...], jnp.concatenate([signal, signal], 0))
        turn_real, turn_imag = turn_ref[0], turn_ref[1]
        turned = []
        for c in range(4):
            real, imag = tile(stage[:TOK], c), tile(stage[TOK:], c)
            turned.append(jnp.concatenate(
                [real * turn_real - imag * turn_imag, real * turn_imag + imag * turn_real], 1
            ))
        return times(jnp.concatenate(turned, 0), second_ref)

    gathered(send_f, recv_f, 0)
    flat_f[...] = recv_f[...].astype(F32).reshape(CHIPS * 2 * OWN, TOK)
    for g in range(2):
        spectrum[g] = forward(flat_f, 4 * g)
    weight_step(1, 0)
    gathered(send_g, recv_g, 1)
    flat_g[...] = recv_g[...].astype(F32).reshape(CHIPS * 2 * OWN, TOK)

    def convolve(g):
        signal = forward(flat_g, 4 * g)
        other = spectrum[g]
        real, imag = tile(signal, 0), tile(signal, 1)
        other_real, other_imag = tile(other, 0), tile(other, 1)
        joint = jnp.concatenate(
            [real * other_real - imag * other_imag, real * other_imag + imag * other_real], 1
        )
        mixed = times(joint, third_ref)
        turn_real, turn_imag = turn_ref[0], turn_ref[1]
        back = []
        for c in range(4):
            rows = mixed[TOK * c : TOK * c + TOK]
            real, imag = tile(rows, 0), tile(rows, 1)
            back.append(jnp.concatenate(
                [real * turn_real + imag * turn_imag, imag * turn_real - real * turn_imag], 0
            ))
        high, low = halves(jnp.concatenate(back, 1))
        result = dot(last_ref[0], high) + dot(last_ref[0], low) + dot(last_ref[1], high)
        for c in range(4):
            flat_y[pl.ds(4 * g + c, TOK, stride=OWN), :] = tile(result, c)

    weight_step(1, 1)
    convolve(0)
    weight_step(2, 0)
    convolve(1)
    weight_step(2, 1)
    exr_out[...] = ys[:, o].reshape(CHIPS * OWN, TOK).astype(BF16)
    swap_r = remote(exr_out, exr_in, ex_send.at[2], ex_recv.at[2], {"ctx": partner})
    swap_r.start()
    swap_r.wait()
    ys[:, o] = exr_in[...].astype(F32).reshape(CHIPS, OWN, TOK)
    send_r[...] = ys[...].reshape(CHIPS, 2 * OWN, TOK).astype(BF16)
    spread(send_r, recv_r, 2)
    weight_step(3, 0)
    gathered(send_r, recv_r, 2)
    weight_step(3, 1)
    for j in range(WIDTH // 128):
        lanes = slice(128 * j, 128 * j + 128)
        block = recv_r[8 * j : 8 * j + 8].astype(F32).reshape(128, TOK).T
        hidden[:, lanes] = (v_ref[:, lanes].astype(F32) * block).astype(BF16)
    weight_step(4, 0)
    def project(block, t, r):
        rows = wall[2 * block + t, :, :, r].reshape(256, WIDTH)
        return lax.dot_general(
            hidden[...], rows, (((1,), (1,)), ((), ())), preferred_element_type=F32
        )

    def hop(r, t):
        return remote(
            hop_out.at[r, t], hop_in.at[r, t], x_send.at[r, t], x_recv.at[r, t],
            {"ch": x_left if t else x_right},
        )

    def share_of(r, side):
        return remote(
            left_out.at[r] if side else right_out.at[r],
            from_right.at[r] if side else from_left.at[r],
            x_send.at[r, 2 + side], x_recv.at[r, 2 + side], {"ch": x_left if side else x_right},
        )

    def far(r):
        for t in range(2):
            hop_out[r, t] = project((x + 2) % NX, t, r).astype(BF16)
            hop(r, t).start()

    def near(r):
        right_out[r, 1] = project(x_right, 1, r).astype(BF16)
        left_out[r, 0] = project(x_left, 0, r).astype(BF16)
        part_r[r] = project(x_right, 0, r)
        part_l[r] = project(x_left, 1, r)

    def onward(r):
        hop(r, 0).wait()
        right_out[r, 0] = (part_r[r] + hop_in[r, 0].astype(F32)).astype(BF16)
        share_of(r, 0).start()
        hop(r, 1).wait()
        left_out[r, 1] = (part_l[r] + hop_in[r, 1].astype(F32)).astype(BF16)
        share_of(r, 1).start()

    arrived(wall.at[:, :, o, 0], wp_recv.at[0])
    far(0)
    near(0)
    onward(0)
    weight_step(4, 1)
    arrived(wall.at[:, :, o, 1], wp_recv.at[1])
    far(1)
    near(1)
    mine = [[project(x, t, 0) for t in range(2)]]
    onward(1)
    mine.append([project(x, t, 1) for t in range(2)])
    for r in range(2):
        for side in range(2):
            share_of(r, side).wait()
    for t in range(2):
        pieces = [
            (mine[r][t] + from_left[r, t].astype(F32) + from_right[r, t].astype(F32)).astype(BF16)
            for r in range(2)
        ]
        out_ref[:, 512 * t : 512 * t + 512] = dot(jnp.concatenate(pieces, 1), order_ref[...]).astype(BF16)

    arrived(wall.at[0, pl.ds(0, 7), s], w1_send)
    arrived(wall.at[pl.ds(0, 7), :, s], w2_send)
    arrived(wall.at[:, :, s], wp_send)


def local(query_act, key_act, value_act, short_filter, long_filter, out_weight):
    tables = make_tables()
    vmem = pl.BlockSpec(memory_space=pltpu.VMEM)
    rows = CHIPS * OWN
    block_f32 = pltpu.VMEM((CHIPS, 2, OWN, TOK), F32)
    half_bf16 = pltpu.VMEM((rows, TOK), BF16)
    tiles = pltpu.VMEM((CHIPS, 2 * OWN, TOK), BF16)
    act = pltpu.VMEM((TOK, WIDTH), BF16)
    lane_tiles = pltpu.VMEM((WIDTH // 128, TOK, 128), BF16)
    share_bf16 = pltpu.VMEM((2, 2, TOK, 256), BF16)
    share_f32 = pltpu.VMEM((2, TOK, 256), F32)
    dma = pltpu.SemaphoreType.DMA
    return pl.pallas_call(
        kernel,
        out_shape=jax.ShapeDtypeStruct((TOK, WIDTH), BF16),
        in_specs=[pl.BlockSpec(memory_space=pl.ANY)] * (6 + len(tables)),
        out_specs=vmem,
        scratch_shapes=[
            act, act, act, pltpu.VMEM((TOK, WIDTH), F32), pltpu.VMEM((TOK, WIDTH), F32),
            *[pltpu.VMEM(table.shape, table.dtype) for table in tables], dma((11,)),
            pltpu.VMEM((WIDTH // 128, 2 * TOK, 128), F32), pltpu.VMEM((WIDTH // 128, TOK, 128), F32),
            lane_tiles, lane_tiles,
            block_f32, block_f32, block_f32,
            half_bf16, half_bf16, half_bf16, half_bf16, half_bf16, half_bf16,
            tiles, tiles, tiles, tiles, tiles, tiles,
            pltpu.VMEM((2, 4 * TOK, 2 * TOK), F32),
            pltpu.VMEM((NY, NZ, 2, 2, 16, WIDTH), BF16),
            act,
            share_bf16, share_bf16, share_bf16, share_bf16, share_bf16, share_bf16,
            share_f32, share_f32,
            dma((4,)), dma((4,)), dma((3,)), dma((3,)), dma, dma((2, 2)), dma, dma((2, 2, 4, 2)), dma, dma((2,)),
            dma((2, 4)), dma((2, 4)),
        ],
        compiler_params=pltpu.CompilerParams(
            collective_id=0, has_side_effects=True, vmem_limit_bytes=60 * 1024 * 1024
        ),
    )(query_act, key_act, value_act, short_filter, long_filter, out_weight.T, *tables)


def solution(mesh):
    placed = (
        P("ctx", "ch"),
        P("ctx", "ch"),
        P("ctx", "ch"),
        P(None, "ch"),
        P("ctx", "ch"),
        P("ch", "ctx"),
    )
    return jax.shard_map(
        local, mesh=mesh, in_specs=placed, out_specs=P("ctx", "ch"), check_vma=False
    )
```

```python
import math

import jax
import jax.numpy as jnp
import numpy as np
from jax import lax
from jax.experimental import pallas as pl
from jax.experimental.pallas import tpu as pltpu
from jax.sharding import PartitionSpec as P

NX, NY, NZ = 4, 8, 8
CHIPS = NY * NZ
TOK = 128
WIDTH = 1024
OWN = 8
MESH = pl.DeviceIdType.MESH
F32, BF16 = jnp.float32, jnp.bfloat16


def split_table(table):
    high = table.astype(jnp.bfloat16)
    low = (table - high.astype(np.float64)).astype(jnp.bfloat16)
    return high, low


def make_tables():
    blocks = 2 * CHIPS
    half_odd = np.arange(blocks) + 0.5
    index = np.arange(blocks)
    angle = 2 * math.pi * half_odd[:, None] * index[None, :] / (2 * blocks)
    first = np.concatenate([np.cos(angle), -np.sin(angle)], 0)
    fold = split_table(first)
    first_cat = np.concatenate(fold, 1)
    last = split_table(first.T * (2.0 / (2 * blocks * TOK)))
    inner = 2 * math.pi * (np.arange(TOK)[:, None] * np.arange(TOK)[None, :] % TOK) / TOK
    cosine, minus_sine = np.cos(inner), -np.sin(inner)
    second = np.block([[cosine, minus_sine], [-minus_sine, cosine]])
    second_split = split_table(second)
    third_split = split_table(second.T)
    turn = 2 * math.pi * half_odd[:, None] * np.arange(TOK)[None, :] / (2 * blocks * TOK)
    order = np.zeros((512, 512))
    column = np.arange(512)
    lane = column // 16 % 2 * 256 + column // 32 % 2 * 128 + column // 64 * 16 + column % 16
    order[lane, column] = 1.0
    return (
        first_cat,
        np.stack(last),
        np.stack(second_split),
        np.stack(third_split),
        np.stack([np.cos(turn), -np.sin(turn)]).astype(np.float32),
        order.astype(jnp.bfloat16),
    )


def dot(a, b):
    return jnp.dot(a, b, preferred_element_type=F32)


def halves(value):
    high = value.astype(BF16)
    return high, (value - high.astype(F32)).astype(BF16)


def kernel(
    q_hbm, k_hbm, v_hbm, sf_hbm, lf_hbm, wt_ref,
    first_hbm, last_hbm, second_hbm, third_hbm, turn_hbm, order_hbm,
    out_ref,
    q_ref, k_ref, v_ref, sf_ref, lf_ref,
    first_ref, last_ref, second_ref, third_ref, turn_ref, order_ref, load_sems,
    ext, short, halo_out, halo_in,
    tf, tg, ys,
    exf_out, exf_in, exg_out, exg_in, exr_out, exr_in,
    send_f, recv_f, send_g, recv_g, send_r, recv_r,
    spectrum, wall, hidden,
    hop_out, hop_in, right_out, left_out, from_left, from_right, part_r, part_l,
    ex_send, ex_recv, a_send, a_recv, w1_send, w1_recv, w2_send, w2_recv, wp_send, wp_recv,
    x_send, x_recv,
):
    me = lax.axis_index("ctx")
    x = lax.axis_index("ch")
    m, s = me // 2, me % 2
    o = 1 - s
    y, z = m // NZ, m % NZ
    partner = 2 * m + o
    after = (me + 1) % (2 * CHIPS)
    x_right, x_left = (x + 1) % NX, (x + NX - 1) % NX

    def plane(chip):
        return {"ctx": 2 * chip + s}

    loads = [
        pltpu.make_async_copy(src, dst, load_sems.at[i])
        for i, (src, dst) in enumerate([
            (k_hbm, k_ref), (v_hbm, v_ref), (lf_hbm, lf_ref), (sf_hbm, sf_ref), (q_hbm, q_ref),
            (first_hbm, first_ref), (second_hbm, second_ref), (turn_hbm, turn_ref),
            (third_hbm, third_ref), (last_hbm, last_ref), (order_hbm, order_ref),
        ])
    ]
    for load in loads:
        load.start()

    barrier = pltpu.get_barrier_semaphore()

    def greet(i, carry):
        pl.semaphore_signal(barrier, inc=1, device_id=plane((m + i) % CHIPS), device_id_type=MESH)
        return carry

    lax.fori_loop(1, CHIPS, greet, 0)
    other_chip = (m + 2 * s - 1 + CHIPS) % CHIPS
    for device in (
        {"ctx": partner}, {"ctx": 2 * other_chip + o}, {"ch": x_right}, {"ch": x_left},
    ):
        pl.semaphore_signal(barrier, inc=1, device_id=device, device_id_type=MESH)

    def remote(src, dst, send, recv, device):
        return pltpu.make_async_remote_copy(
            src_ref=src, dst_ref=dst, send_sem=send, recv_sem=recv,
            device_id=device, device_id_type=MESH,
        )

    def arrived(ref, sem):
        pltpu.make_async_copy(ref, ref, sem).wait()

    y_right, y_left = (y + 1) % NY, (y + NY - 1) % NY
    z_right, z_left = (z + 1) % NZ, (z + NZ - 1) % NZ

    def chunk(h, offset, r, part=None):
        span = slice(None) if part is None else pl.ds(4 * part, 4)
        if h == 0:
            return wall.at[s, r, 0, (y + offset + NY) % NY, span]
        return wall.at[s, r, 1, span, (z + offset + NZ) % NZ]

    def piece(h, offset, r):
        if h == 0:
            return wall.at[s, r, 0, y, (z + offset + NZ) % NZ]
        return wall.at[s, r, 1, (y + offset + NY) % NY, z]

    def toward(h, right):
        if h == 0:
            return plane((y_right if right else y_left) * NZ + z)
        return plane(y * NZ + (z_right if right else z_left))

    def share(ref, r):
        remote(ref, ref, wp_send, wp_recv.at[r], {"ctx": partner}).start()

    def beside(h, step):
        if h == 0:
            return plane(y * NZ + (z + step + NZ) % NZ)
        return plane((y + step + NY) % NY * NZ + z)

    def weight_start():
        for r in range(2):
            for h in range(2):
                own, place = wt_ref.at[pl.ds(16 * r, 16), pl.ds(512 * h, 512)], piece(h, 0, r)
                pltpu.make_async_copy(own, place, w1_recv.at[r, h, 0]).start()
                for step, which in ((2, 1), (-2, 2), (1, 0), (-1, 0)):
                    remote(own, place, w1_send, w1_recv.at[r, h, which], beside(h, step)).start()

    def weight_relay():
        for r in range(2):
            for h in range(2):
                for step, which, targets in ((-2, 1, (2, 1)), (2, 2, (-1,))):
                    moved = piece(h, step, r)
                    arrived(moved, w1_recv.at[r, h, which])
                    for target in targets:
                        remote(moved, moved, w1_send, w1_recv.at[r, h, 0], beside(h, target)).start()

    def weight_step(j, r):
        for h in range(2):
            if j == 0:
                arrived(wall.at[s, r, h, 0, pl.ds(0, 6)], w1_recv.at[r, h, 0])
            elif j < 4:
                arrived(chunk(h, -j, r), w2_recv.at[h, 0, j - 1, r])
                arrived(chunk(h, j, r), w2_recv.at[h, 1, j - 1, r])
            else:
                arrived(chunk(h, 4, r, 0), w2_recv.at[h, 0, 3, r])
                arrived(chunk(h, 4, r, 1), w2_recv.at[h, 1, 3, r])
                share(chunk(h, 4, r), r)
            if j < 4:
                for side in range(2):
                    moved = chunk(h, j if side else -j, r, side if j == 3 else None)
                    remote(
                        moved, moved, w2_send, w2_recv.at[h, side, j, r], toward(h, side == 0)
                    ).start()
            if j == 0:
                share(chunk(h, 0, r), r)
            elif j < 4:
                share(chunk(h, -j, r), r)
                share(chunk(h, j, r), r)

    loads[0].wait()
    loads[1].wait()
    for j in range(WIDTH // 128):
        lanes = slice(128 * j, 128 * j + 128)
        product = k_ref[:, lanes].astype(F32) * v_ref[:, lanes].astype(F32)
        ext[j, TOK:] = product
        halo_out[j] = product.astype(BF16)

    loads[2].wait()
    for j in range(WIDTH // 128):
        lanes = slice(128 * j, 128 * j + 128)
        tf[8 * j : 8 * j + 8] = lf_ref[:, lanes].T.reshape(8, 2, OWN, TOK)
    exf_out[...] = tf[:, o].reshape(CHIPS * OWN, TOK).astype(BF16)
    loads[3].wait()

    def short_part(j, prior):
        lanes = pl.ds(pl.multiple_of(j * 128, 128), 128)
        if prior:
            accum = [short[j, 8 * i : 8 * i + 8] for i in range(16)]
        else:
            accum = [jnp.zeros((8, 128), F32) for i in range(16)]
        for r in range(8):
            ranks = range(1, 17) if prior else range(17, 32)
            windows = {u: ext[j, 8 * u - r : 8 * u - r + 8] for u in ranks}
            for q in range(16):
                taps = jnp.broadcast_to(sf_ref[8 * q + r : 8 * q + r + 1, lanes], (8, 128))
                for i in range(0, q + 1) if prior else range(q + 1, 16):
                    accum[i] = accum[i] + taps * windows[i - q + 16]
        for i in range(16):
            short[j, 8 * i : 8 * i + 8] = accum[i]

    def short_own(j, carry):
        short_part(j, False)
        return carry

    def short_prior(j, carry):
        short_part(j, True)
        return carry

    lax.fori_loop(0, WIDTH // 128, short_own, 0)

    pl.semaphore_wait(barrier, CHIPS + 3)

    halo = remote(halo_out, halo_in, ex_send.at[1], ex_recv.at[1], {"ctx": after})
    halo.start()
    weight_start()

    swap_f = remote(exf_out, exf_in, ex_send.at[0], ex_recv.at[0], {"ctx": partner})
    swap_f.start()

    def spread(src, dst, which):
        pltpu.make_async_copy(src.at[m], dst.at[m], a_recv.at[which]).start()

        def one(i, carry):
            chip = (m + i) % CHIPS
            remote(src.at[chip], dst.at[m], a_send.at[which], a_recv.at[which], plane(chip)).start()
            return carry

        lax.fori_loop(1, CHIPS, one, 0)

    def gathered(src, dst, which):
        arrived(dst, a_recv.at[which])

    swap_f.wait_recv()
    tf[:, o] = exf_in[...].astype(F32).reshape(CHIPS, OWN, TOK)
    send_f[...] = tf[...].reshape(CHIPS, 2 * OWN, TOK).astype(BF16)
    weight_relay()
    spread(send_f, recv_f, 0)
    halo.wait_recv()
    loads[4].wait()
    first_device = me == 0
    for j in range(WIDTH // 128):
        ext[j, :TOK] = jnp.where(first_device, 0.0, halo_in[j].astype(F32))
    lax.fori_loop(0, WIDTH // 128, short_prior, 0)
    for j in range(WIDTH // 128):
        lanes = slice(128 * j, 128 * j + 128)
        tg[8 * j : 8 * j + 8] = (q_ref[:, lanes].astype(F32) * short[j]).T.reshape(8, 2, OWN, TOK)
    exg_out[...] = tg[:, o].reshape(CHIPS * OWN, TOK).astype(BF16)
    swap_g = remote(exg_out, exg_in, ex_send.at[3], ex_recv.at[3], {"ctx": partner})
    swap_g.start()
    weight_step(0, 0)
    swap_g.wait_recv()
    tg[:, o] = exg_in[...].astype(F32).reshape(CHIPS, OWN, TOK)
    send_g[...] = tg[...].reshape(CHIPS, 2 * OWN, TOK).astype(BF16)
    spread(send_g, recv_g, 1)
    weight_step(0, 1)
    for load in loads[5:]:
        load.wait()
    flat_f = tf.reshape(CHIPS * 2 * OWN, TOK)
    flat_g = tg.reshape(CHIPS * 2 * OWN, TOK)
    flat_y = ys.reshape(CHIPS * 2 * OWN, TOK)

    def tile(value, c):
        return value[:, TOK * c : TOK * c + TOK]

    def times(value, table):
        high, low = halves(value)
        return dot(high, table[0]) + dot(low, table[0]) + dot(high, table[1])

    def forward(flat, base):
        signal = jnp.concatenate(
            [flat[pl.ds(base + c, TOK, stride=OWN), :].astype(BF16) for c in range(4)], 1
        )
        stage = dot(first_ref[...], jnp.concatenate([signal, signal], 0))
        turn_real, turn_imag = turn_ref[0], turn_ref[1]
        turned = []
        for c in range(4):
            real, imag = tile(stage[:TOK], c), tile(stage[TOK:], c)
            turned.append(jnp.concatenate(
                [real * turn_real - imag * turn_imag, real * turn_imag + imag * turn_real], 1
            ))
        return times(jnp.concatenate(turned, 0), second_ref)

    gathered(send_f, recv_f, 0)
    flat_f[...] = recv_f[...].astype(F32).reshape(CHIPS * 2 * OWN, TOK)
    for g in range(2):
        spectrum[g] = forward(flat_f, 4 * g)
    weight_step(1, 0)
    gathered(send_g, recv_g, 1)
    flat_g[...] = recv_g[...].astype(F32).reshape(CHIPS * 2 * OWN, TOK)

    def convolve(g):
        signal = forward(flat_g, 4 * g)
        other = spectrum[g]
        real, imag = tile(signal, 0), tile(signal, 1)
        other_real, other_imag = tile(other, 0), tile(other, 1)
        joint = jnp.concatenate(
            [real * other_real - imag * other_imag, real * other_imag + imag * other_real], 1
        )
        mixed = times(joint, third_ref)
        turn_real, turn_imag = turn_ref[0], turn_ref[1]
        back = []
        for c in range(4):
            rows = mixed[TOK * c : TOK * c + TOK]
            real, imag = tile(rows, 0), tile(rows, 1)
            back.append(jnp.concatenate(
                [real * turn_real + imag * turn_imag, imag * turn_real - real * turn_imag], 0
            ))
        high, low = halves(jnp.concatenate(back, 1))
        result = dot(last_ref[0], high) + dot(last_ref[0], low) + dot(last_ref[1], high)
        for c in range(4):
            flat_y[pl.ds(4 * g + c, TOK, stride=OWN), :] = tile(result, c)

    weight_step(1, 1)
    convolve(0)
    weight_step(2, 0)
    convolve(1)
    weight_step(2, 1)
    exr_out[...] = ys[:, o].reshape(CHIPS * OWN, TOK).astype(BF16)
    swap_r = remote(exr_out, exr_in, ex_send.at[2], ex_recv.at[2], {"ctx": partner})
    swap_r.start()
    swap_r.wait_recv()
    ys[:, o] = exr_in[...].astype(F32).reshape(CHIPS, OWN, TOK)
    send_r[...] = ys[...].reshape(CHIPS, 2 * OWN, TOK).astype(BF16)
    spread(send_r, recv_r, 2)
    weight_step(3, 0)
    gathered(send_r, recv_r, 2)
    weight_step(3, 1)
    for j in range(WIDTH // 128):
        lanes = slice(128 * j, 128 * j + 128)
        block = recv_r[8 * j : 8 * j + 8].astype(F32).reshape(128, TOK).T
        hidden[:, lanes] = (v_ref[:, lanes].astype(F32) * block).astype(BF16)
    weight_step(4, 0)
    def project(block, t, r):
        return sum(
            lax.dot_general(
                hidden[:, 512 * h : 512 * h + 512], wall[:, r, h, 2 * block + t].reshape(256, 512),
                (((1,), (1,)), ((), ())), preferred_element_type=F32,
            )
            for h in range(2)
        )

    def hop(r, t):
        return remote(
            hop_out.at[r, t], hop_in.at[r, t], x_send.at[r, t], x_recv.at[r, t],
            {"ch": x_left if t else x_right},
        )

    def share_of(r, side, t):
        return remote(
            (left_out if side else right_out).at[r, t], (from_right if side else from_left).at[r, t],
            x_send.at[r, 2 + 2 * side + t], x_recv.at[r, 2 + 2 * side + t],
            {"ch": x_left if side else x_right},
        )

    def far(r):
        for t in range(2):
            hop_out[r, t] = project((x + 2) % NX, t, r).astype(BF16)
            hop(r, t).start()

    def near(r):
        right_out[r, 1] = project(x_right, 1, r).astype(BF16)
        share_of(r, 0, 1).start()
        left_out[r, 0] = project(x_left, 0, r).astype(BF16)
        share_of(r, 1, 0).start()
        part_r[r] = project(x_right, 0, r)
        part_l[r] = project(x_left, 1, r)

    def onward(r):
        hop(r, 0).wait_recv()
        right_out[r, 0] = (part_r[r] + hop_in[r, 0].astype(F32)).astype(BF16)
        share_of(r, 0, 0).start()
        hop(r, 1).wait_recv()
        left_out[r, 1] = (part_l[r] + hop_in[r, 1].astype(F32)).astype(BF16)
        share_of(r, 1, 1).start()

    def total_of(r, own):
        for side in range(2):
            for t in range(2):
                share_of(r, side, t).wait_recv()
        return [
            dot(
                (own[t] + from_left[r, t].astype(F32) + from_right[r, t].astype(F32)).astype(BF16),
                order_ref[256 * r : 256 * r + 256],
            )
            for t in range(2)
        ]

    arrived(wall.at[o, 0], wp_recv.at[0])
    far(0)
    near(0)
    onward(0)
    weight_step(4, 1)
    arrived(wall.at[o, 1], wp_recv.at[1])
    far(1)
    near(1)
    own_first = [project(x, t, 0) for t in range(2)]
    onward(1)
    own_second = [project(x, t, 1) for t in range(2)]
    first = total_of(0, own_first)
    second = total_of(1, own_second)
    for t in range(2):
        out_ref[:, 512 * t : 512 * t + 512] = (first[t] + second[t]).astype(BF16)

    for copy in (swap_f, swap_g, swap_r, halo):
        copy.wait_send()
    for which, src in enumerate((send_f, send_g, send_r)):
        arrived(src.at[pl.ds(0, CHIPS - 1)], a_send.at[which])
    for r in range(2):
        for t in range(2):
            hop(r, t).wait_send()
            for side in range(2):
                share_of(r, side, t).wait_send()
    arrived(wall.at[0, 0, 0, pl.ds(0, 7), pl.ds(0, 4)], w1_send)
    arrived(wall.at[0, :, :, pl.ds(0, 7)], w2_send)
    arrived(wall.at[s], wp_send)


def local(query_act, key_act, value_act, short_filter, long_filter, out_weight):
    tables = make_tables()
    vmem = pl.BlockSpec(memory_space=pltpu.VMEM)
    rows = CHIPS * OWN
    block_f32 = pltpu.VMEM((CHIPS, 2, OWN, TOK), F32)
    half_bf16 = pltpu.VMEM((rows, TOK), BF16)
    tiles = pltpu.VMEM((CHIPS, 2 * OWN, TOK), BF16)
    act = pltpu.VMEM((TOK, WIDTH), BF16)
    lane_tiles = pltpu.VMEM((WIDTH // 128, TOK, 128), BF16)
    share_bf16 = pltpu.VMEM((2, 2, TOK, 256), BF16)
    share_f32 = pltpu.VMEM((2, TOK, 256), F32)
    dma = pltpu.SemaphoreType.DMA
    return pl.pallas_call(
        kernel,
        out_shape=jax.ShapeDtypeStruct((TOK, WIDTH), BF16),
        in_specs=[pl.BlockSpec(memory_space=pl.ANY)] * (6 + len(tables)),
        out_specs=vmem,
        scratch_shapes=[
            act, act, act, pltpu.VMEM((TOK, WIDTH), F32), pltpu.VMEM((TOK, WIDTH), F32),
            *[pltpu.VMEM(table.shape, table.dtype) for table in tables], dma((11,)),
            pltpu.VMEM((WIDTH // 128, 2 * TOK, 128), F32), pltpu.VMEM((WIDTH // 128, TOK, 128), F32),
            lane_tiles, lane_tiles,
            block_f32, block_f32, block_f32,
            half_bf16, half_bf16, half_bf16, half_bf16, half_bf16, half_bf16,
            tiles, tiles, tiles, tiles, tiles, tiles,
            pltpu.VMEM((2, 4 * TOK, 2 * TOK), F32),
            pltpu.VMEM((2, 2, 2, NY, NZ, 16, WIDTH // 2), BF16),
            act,
            share_bf16, share_bf16, share_bf16, share_bf16, share_bf16, share_bf16,
            share_f32, share_f32,
            dma((4,)), dma((4,)), dma((3,)), dma((3,)), dma, dma((2, 2, 3)), dma, dma((2, 2, 4, 2)), dma, dma((2,)),
            dma((2, 6)), dma((2, 6)),
        ],
        compiler_params=pltpu.CompilerParams(
            collective_id=0, has_side_effects=True, vmem_limit_bytes=60 * 1024 * 1024
        ),
    )(query_act, key_act, value_act, short_filter, long_filter, out_weight.T, *tables)


def solution(mesh):
    placed = (
        P("ctx", "ch"),
        P("ctx", "ch"),
        P("ctx", "ch"),
        P(None, "ch"),
        P("ctx", "ch"),
        P("ch", "ctx"),
    )
    return jax.shard_map(
        local, mesh=mesh, in_specs=placed, out_specs=P("ctx", "ch"), check_vma=False
    )
```

```python
import math

import jax
import jax.numpy as jnp
import numpy as np
from jax import lax
from jax.experimental import pallas as pl
from jax.experimental.pallas import tpu as pltpu
from jax.sharding import PartitionSpec as P

NX, NY, NZ = 4, 8, 8
CHIPS = NY * NZ
TOK = 128
WIDTH = 1024
OWN = 8
MESH = pl.DeviceIdType.MESH
F32, BF16 = jnp.float32, jnp.bfloat16


def split_table(table):
    high = table.astype(jnp.bfloat16)
    low = (table - high.astype(np.float64)).astype(jnp.bfloat16)
    return high, low


def make_tables():
    blocks = 2 * CHIPS
    half_odd = np.arange(blocks) + 0.5
    index = np.arange(blocks)
    angle = 2 * math.pi * half_odd[:, None] * index[None, :] / (2 * blocks)
    first = np.concatenate([np.cos(angle), -np.sin(angle)], 0)
    fold = split_table(first)
    first_cat = np.concatenate(fold, 1)
    last = split_table(first.T * (2.0 / (2 * blocks * TOK)))
    inner = 2 * math.pi * (np.arange(TOK)[:, None] * np.arange(TOK)[None, :] % TOK) / TOK
    cosine, minus_sine = np.cos(inner), -np.sin(inner)
    second = np.block([[cosine, minus_sine], [-minus_sine, cosine]])
    second_split = split_table(second)
    third_split = split_table(second.T)
    turn = 2 * math.pi * half_odd[:, None] * np.arange(TOK)[None, :] / (2 * blocks * TOK)
    order = np.zeros((512, 512))
    column = np.arange(512)
    lane = column // 16 % 2 * 256 + column // 32 % 2 * 128 + column // 64 * 16 + column % 16
    order[lane, column] = 1.0
    return (
        first_cat,
        np.stack(last),
        np.stack(second_split),
        np.stack(third_split),
        np.stack([np.cos(turn), -np.sin(turn)]).astype(np.float32),
        order.astype(jnp.bfloat16),
    )


def dot(a, b):
    return jnp.dot(a, b, preferred_element_type=F32)


def halves(value):
    high = value.astype(BF16)
    return high, (value - high.astype(F32)).astype(BF16)


def kernel(
    q_hbm, k_hbm, v_hbm, sf_hbm, lf_hbm, wt_ref,
    first_hbm, last_hbm, second_hbm, third_hbm, turn_hbm, order_hbm,
    out_ref,
    q_ref, k_ref, v_ref, sf_ref, lf_ref,
    first_ref, last_ref, second_ref, third_ref, turn_ref, order_ref, load_sems,
    ext, short, halo_out, halo_in,
    tf, tg, ys,
    exf_out, exf_in, exg_out, exg_in, exr_out, exr_in,
    send_f, recv_f, send_g, recv_g, send_r, recv_r,
    spectrum, wall, hidden,
    hop_out, hop_in, right_out, left_out, from_left, from_right, part_r, part_l,
    ex_send, ex_recv, a_send, a_recv, w1_send, w1_recv, w2_send, w2_recv, wp_send, wp_recv,
    x_send, x_recv,
):
    me = lax.axis_index("ctx")
    x = lax.axis_index("ch")
    m, s = me // 2, me % 2
    o = 1 - s
    y, z = m // NZ, m % NZ
    partner = 2 * m + o
    after = (me + 1) % (2 * CHIPS)
    x_right, x_left = (x + 1) % NX, (x + NX - 1) % NX

    def plane(chip):
        return {"ctx": 2 * chip + s}

    loads = [
        pltpu.make_async_copy(src, dst, load_sems.at[i])
        for i, (src, dst) in enumerate([
            (k_hbm, k_ref), (v_hbm, v_ref), (lf_hbm, lf_ref), (sf_hbm, sf_ref), (q_hbm, q_ref),
            (first_hbm, first_ref), (second_hbm, second_ref), (turn_hbm, turn_ref),
            (third_hbm, third_ref), (last_hbm, last_ref), (order_hbm, order_ref),
        ])
    ]
    for load in loads:
        load.start()

    barrier = pltpu.get_barrier_semaphore()

    def greet(i, carry):
        pl.semaphore_signal(barrier, inc=1, device_id=plane((m + i) % CHIPS), device_id_type=MESH)
        return carry

    lax.fori_loop(1, CHIPS, greet, 0)
    other_chip = (m + 2 * s - 1 + CHIPS) % CHIPS
    for device in (
        {"ctx": partner}, {"ctx": 2 * other_chip + o}, {"ch": x_right}, {"ch": x_left},
    ):
        pl.semaphore_signal(barrier, inc=1, device_id=device, device_id_type=MESH)

    def remote(src, dst, send, recv, device):
        return pltpu.make_async_remote_copy(
            src_ref=src, dst_ref=dst, send_sem=send, recv_sem=recv,
            device_id=device, device_id_type=MESH,
        )

    def arrived(ref, sem):
        pltpu.make_async_copy(ref, ref, sem).wait()

    y_right, y_left = (y + 1) % NY, (y + NY - 1) % NY
    z_right, z_left = (z + 1) % NZ, (z + NZ - 1) % NZ

    def chunk(h, offset, r, part=None):
        span = slice(None) if part is None else pl.ds(4 * part, 4)
        if h == 0:
            return wall.at[s, r, 0, (y + offset + NY) % NY, span]
        return wall.at[s, r, 1, span, (z + offset + NZ) % NZ]

    def piece(h, offset, r):
        if h == 0:
            return wall.at[s, r, 0, y, (z + offset + NZ) % NZ]
        return wall.at[s, r, 1, (y + offset + NY) % NY, z]

    def toward(h, right):
        if h == 0:
            return plane((y_right if right else y_left) * NZ + z)
        return plane(y * NZ + (z_right if right else z_left))

    def share(ref, r):
        remote(ref, ref, wp_send, wp_recv.at[r], {"ctx": partner}).start()

    def beside(h, step):
        if h == 0:
            return plane(y * NZ + (z + step + NZ) % NZ)
        return plane((y + step + NY) % NY * NZ + z)

    def weight_start():
        for r in range(2):
            for h in range(2):
                own, place = wt_ref.at[pl.ds(16 * r, 16), pl.ds(512 * h, 512)], piece(h, 0, r)
                pltpu.make_async_copy(own, place, w1_recv.at[r, h, 0]).start()
                for step, which in ((2, 1), (-2, 2), (1, 0), (-1, 0)):
                    remote(own, place, w1_send, w1_recv.at[r, h, which], beside(h, step)).start()

    def weight_relay():
        for r in range(2):
            for h in range(2):
                for step, which, targets in ((-2, 1, (2, 1)), (2, 2, (-1,))):
                    moved = piece(h, step, r)
                    arrived(moved, w1_recv.at[r, h, which])
                    for target in targets:
                        remote(moved, moved, w1_send, w1_recv.at[r, h, 0], beside(h, target)).start()

    def weight_step(j, r):
        for h in range(2):
            if j == 0:
                arrived(wall.at[s, r, h, 0, pl.ds(0, 6)], w1_recv.at[r, h, 0])
            elif j < 4:
                arrived(chunk(h, -j, r), w2_recv.at[h, 0, j - 1, r])
                arrived(chunk(h, j, r), w2_recv.at[h, 1, j - 1, r])
            else:
                arrived(chunk(h, 4, r, 0), w2_recv.at[h, 0, 3, r])
                arrived(chunk(h, 4, r, 1), w2_recv.at[h, 1, 3, r])
            if j < 4:
                for side in range(2):
                    moved = chunk(h, j if side else -j, r, side if j == 3 else None)
                    remote(
                        moved, moved, w2_send, w2_recv.at[h, side, j, r], toward(h, side == 0)
                    ).start()
        for h in range(2):
            if j == 0:
                share(chunk(h, 0, r), r)
            elif j < 4:
                share(chunk(h, -j, r), r)
                share(chunk(h, j, r), r)
            else:
                share(chunk(h, 4, r), r)

    loads[0].wait()
    loads[1].wait()
    for j in range(WIDTH // 128):
        lanes = slice(128 * j, 128 * j + 128)
        product = k_ref[:, lanes].astype(F32) * v_ref[:, lanes].astype(F32)
        ext[j, TOK:] = product
        halo_out[j] = product.astype(BF16)

    loads[2].wait()
    for j in range(WIDTH // 128):
        lanes = slice(128 * j, 128 * j + 128)
        tf[8 * j : 8 * j + 8] = lf_ref[:, lanes].T.reshape(8, 2, OWN, TOK)
    exf_out[...] = tf[:, o].reshape(CHIPS * OWN, TOK).astype(BF16)
    loads[3].wait()

    def short_part(j, prior):
        lanes = pl.ds(pl.multiple_of(j * 128, 128), 128)
        if prior:
            accum = [short[j, 8 * i : 8 * i + 8] for i in range(16)]
        else:
            accum = [jnp.zeros((8, 128), F32) for i in range(16)]
        for r in range(8):
            ranks = range(1, 17) if prior else range(17, 32)
            windows = {u: ext[j, 8 * u - r : 8 * u - r + 8] for u in ranks}
            for q in range(16):
                taps = jnp.broadcast_to(sf_ref[8 * q + r : 8 * q + r + 1, lanes], (8, 128))
                for i in range(0, q + 1) if prior else range(q + 1, 16):
                    accum[i] = accum[i] + taps * windows[i - q + 16]
        for i in range(16):
            short[j, 8 * i : 8 * i + 8] = accum[i]

    def short_own(j, carry):
        short_part(j, False)
        return carry

    def short_prior(j, carry):
        short_part(j, True)
        return carry

    lax.fori_loop(0, WIDTH // 128, short_own, 0)

    pl.semaphore_wait(barrier, CHIPS + 3)

    halo = remote(halo_out, halo_in, ex_send.at[1], ex_recv.at[1], {"ctx": after})
    halo.start()
    weight_start()

    swap_f = remote(exf_out, exf_in, ex_send.at[0], ex_recv.at[0], {"ctx": partner})
    swap_f.start()

    def spread(src, dst, which):
        pltpu.make_async_copy(src.at[m], dst.at[m], a_recv.at[which]).start()

        def one(i, carry):
            chip = (m + i) % CHIPS
            remote(src.at[chip], dst.at[m], a_send.at[which], a_recv.at[which], plane(chip)).start()
            return carry

        lax.fori_loop(1, CHIPS, one, 0)

    def gathered(src, dst, which):
        arrived(dst, a_recv.at[which])

    swap_f.wait_recv()
    tf[:, o] = exf_in[...].astype(F32).reshape(CHIPS, OWN, TOK)
    send_f[...] = tf[...].reshape(CHIPS, 2 * OWN, TOK).astype(BF16)
    weight_relay()
    spread(send_f, recv_f, 0)
    halo.wait_recv()
    loads[4].wait()
    first_device = me == 0
    for j in range(WIDTH // 128):
        ext[j, :TOK] = jnp.where(first_device, 0.0, halo_in[j].astype(F32))
    lax.fori_loop(0, WIDTH // 128, short_prior, 0)
    for j in range(WIDTH // 128):
        lanes = slice(128 * j, 128 * j + 128)
        tg[8 * j : 8 * j + 8] = (q_ref[:, lanes].astype(F32) * short[j]).T.reshape(8, 2, OWN, TOK)
    exg_out[...] = tg[:, o].reshape(CHIPS * OWN, TOK).astype(BF16)
    swap_g = remote(exg_out, exg_in, ex_send.at[3], ex_recv.at[3], {"ctx": partner})
    swap_g.start()
    weight_step(0, 0)
    swap_g.wait_recv()
    tg[:, o] = exg_in[...].astype(F32).reshape(CHIPS, OWN, TOK)
    send_g[...] = tg[...].reshape(CHIPS, 2 * OWN, TOK).astype(BF16)
    spread(send_g, recv_g, 1)
    weight_step(0, 1)
    for load in loads[5:]:
        load.wait()
    flat_f = tf.reshape(CHIPS * 2 * OWN, TOK)
    flat_g = tg.reshape(CHIPS * 2 * OWN, TOK)
    flat_y = ys.reshape(CHIPS * 2 * OWN, TOK)

    def tile(value, c):
        return value[:, TOK * c : TOK * c + TOK]

    def times(value, table):
        high, low = halves(value)
        return dot(high, table[0]) + dot(low, table[0]) + dot(high, table[1])

    def forward(flat, base):
        signal = jnp.concatenate(
            [flat[pl.ds(base + c, TOK, stride=OWN), :].astype(BF16) for c in range(4)], 1
        )
        stage = dot(first_ref[...], jnp.concatenate([signal, signal], 0))
        turn_real, turn_imag = turn_ref[0], turn_ref[1]
        turned = []
        for c in range(4):
            real, imag = tile(stage[:TOK], c), tile(stage[TOK:], c)
            turned.append(jnp.concatenate(
                [real * turn_real - imag * turn_imag, real * turn_imag + imag * turn_real], 1
            ))
        return times(jnp.concatenate(turned, 0), second_ref)

    gathered(send_f, recv_f, 0)
    flat_f[...] = recv_f[...].astype(F32).reshape(CHIPS * 2 * OWN, TOK)
    for g in range(2):
        spectrum[g] = forward(flat_f, 4 * g)
    weight_step(1, 0)
    gathered(send_g, recv_g, 1)
    flat_g[...] = recv_g[...].astype(F32).reshape(CHIPS * 2 * OWN, TOK)

    def convolve(g):
        signal = forward(flat_g, 4 * g)
        other = spectrum[g]
        real, imag = tile(signal, 0), tile(signal, 1)
        other_real, other_imag = tile(other, 0), tile(other, 1)
        joint = jnp.concatenate(
            [real * other_real - imag * other_imag, real * other_imag + imag * other_real], 1
        )
        mixed = times(joint, third_ref)
        turn_real, turn_imag = turn_ref[0], turn_ref[1]
        back = []
        for c in range(4):
            rows = mixed[TOK * c : TOK * c + TOK]
            real, imag = tile(rows, 0), tile(rows, 1)
            back.append(jnp.concatenate(
                [real * turn_real + imag * turn_imag, imag * turn_real - real * turn_imag], 0
            ))
        high, low = halves(jnp.concatenate(back, 1))
        result = dot(last_ref[0], high) + dot(last_ref[0], low) + dot(last_ref[1], high)
        for c in range(4):
            flat_y[pl.ds(4 * g + c, TOK, stride=OWN), :] = tile(result, c)

    weight_step(1, 1)
    convolve(0)
    weight_step(2, 0)
    convolve(1)
    weight_step(2, 1)
    exr_out[...] = ys[:, o].reshape(CHIPS * OWN, TOK).astype(BF16)
    swap_r = remote(exr_out, exr_in, ex_send.at[2], ex_recv.at[2], {"ctx": partner})
    swap_r.start()
    swap_r.wait_recv()
    ys[:, o] = exr_in[...].astype(F32).reshape(CHIPS, OWN, TOK)
    send_r[...] = ys[...].reshape(CHIPS, 2 * OWN, TOK).astype(BF16)
    spread(send_r, recv_r, 2)
    weight_step(3, 0)
    gathered(send_r, recv_r, 2)
    weight_step(3, 1)
    for j in range(WIDTH // 128):
        lanes = slice(128 * j, 128 * j + 128)
        block = recv_r[8 * j : 8 * j + 8].astype(F32).reshape(128, TOK).T
        hidden[:, lanes] = (v_ref[:, lanes].astype(F32) * block).astype(BF16)
    weight_step(4, 0)
    def project(block, t, r):
        return sum(
            lax.dot_general(
                hidden[:, 512 * h : 512 * h + 512], wall[:, r, h, 2 * block + t].reshape(256, 512),
                (((1,), (1,)), ((), ())), preferred_element_type=F32,
            )
            for h in range(2)
        )

    def hop(r, t):
        return remote(
            hop_out.at[r, t], hop_in.at[r, t], x_send.at[r, t], x_recv.at[r, t],
            {"ch": x_left if t else x_right},
        )

    def share_of(r, side, t):
        return remote(
            (left_out if side else right_out).at[r, t], (from_right if side else from_left).at[r, t],
            x_send.at[r, 2 + 2 * side + t], x_recv.at[r, 2 + 2 * side + t],
            {"ch": x_left if side else x_right},
        )

    def far(r):
        for t in range(2):
            hop_out[r, t] = project((x + 2) % NX, t, r).astype(BF16)
            hop(r, t).start()

    def near(r):
        right_out[r, 1] = project(x_right, 1, r).astype(BF16)
        share_of(r, 0, 1).start()
        left_out[r, 0] = project(x_left, 0, r).astype(BF16)
        share_of(r, 1, 0).start()
        part_r[r] = project(x_right, 0, r)
        part_l[r] = project(x_left, 1, r)

    def onward(r):
        hop(r, 0).wait_recv()
        right_out[r, 0] = (part_r[r] + hop_in[r, 0].astype(F32)).astype(BF16)
        share_of(r, 0, 0).start()
        hop(r, 1).wait_recv()
        left_out[r, 1] = (part_l[r] + hop_in[r, 1].astype(F32)).astype(BF16)
        share_of(r, 1, 1).start()

    def total_of(r, own):
        for side in range(2):
            for t in range(2):
                share_of(r, side, t).wait_recv()
        return [
            dot(
                (own[t] + from_left[r, t].astype(F32) + from_right[r, t].astype(F32)).astype(BF16),
                order_ref[256 * r : 256 * r + 256],
            )
            for t in range(2)
        ]

    arrived(wall.at[o, 0], wp_recv.at[0])
    far(0)
    near(0)
    onward(0)
    weight_step(4, 1)
    arrived(wall.at[o, 1], wp_recv.at[1])
    far(1)
    near(1)
    own_first = [project(x, t, 0) for t in range(2)]
    onward(1)
    own_second = [project(x, t, 1) for t in range(2)]
    first = total_of(0, own_first)
    second = total_of(1, own_second)
    for t in range(2):
        out_ref[:, 512 * t : 512 * t + 512] = (first[t] + second[t]).astype(BF16)

    for copy in (swap_f, swap_g, swap_r, halo):
        copy.wait_send()
    for which, src in enumerate((send_f, send_g, send_r)):
        arrived(src.at[pl.ds(0, CHIPS - 1)], a_send.at[which])
    for r in range(2):
        for t in range(2):
            hop(r, t).wait_send()
            for side in range(2):
                share_of(r, side, t).wait_send()
    arrived(wall.at[0, 0, 0, pl.ds(0, 7), pl.ds(0, 4)], w1_send)
    arrived(wall.at[0, :, :, pl.ds(0, 7)], w2_send)
    arrived(wall.at[s], wp_send)


def local(query_act, key_act, value_act, short_filter, long_filter, out_weight):
    tables = make_tables()
    vmem = pl.BlockSpec(memory_space=pltpu.VMEM)
    rows = CHIPS * OWN
    block_f32 = pltpu.VMEM((CHIPS, 2, OWN, TOK), F32)
    half_bf16 = pltpu.VMEM((rows, TOK), BF16)
    tiles = pltpu.VMEM((CHIPS, 2 * OWN, TOK), BF16)
    act = pltpu.VMEM((TOK, WIDTH), BF16)
    lane_tiles = pltpu.VMEM((WIDTH // 128, TOK, 128), BF16)
    share_bf16 = pltpu.VMEM((2, 2, TOK, 256), BF16)
    share_f32 = pltpu.VMEM((2, TOK, 256), F32)
    dma = pltpu.SemaphoreType.DMA
    return pl.pallas_call(
        kernel,
        out_shape=jax.ShapeDtypeStruct((TOK, WIDTH), BF16),
        in_specs=[pl.BlockSpec(memory_space=pl.ANY)] * (6 + len(tables)),
        out_specs=vmem,
        scratch_shapes=[
            act, act, act, pltpu.VMEM((TOK, WIDTH), F32), pltpu.VMEM((TOK, WIDTH), F32),
            *[pltpu.VMEM(table.shape, table.dtype) for table in tables], dma((11,)),
            pltpu.VMEM((WIDTH // 128, 2 * TOK, 128), F32), pltpu.VMEM((WIDTH // 128, TOK, 128), F32),
            lane_tiles, lane_tiles,
            block_f32, block_f32, block_f32,
            half_bf16, half_bf16, half_bf16, half_bf16, half_bf16, half_bf16,
            tiles, tiles, tiles, tiles, tiles, tiles,
            pltpu.VMEM((2, 4 * TOK, 2 * TOK), F32),
            pltpu.VMEM((2, 2, 2, NY, NZ, 16, WIDTH // 2), BF16),
            act,
            share_bf16, share_bf16, share_bf16, share_bf16, share_bf16, share_bf16,
            share_f32, share_f32,
            dma((4,)), dma((4,)), dma((3,)), dma((3,)), dma, dma((2, 2, 3)), dma, dma((2, 2, 4, 2)), dma, dma((2,)),
            dma((2, 6)), dma((2, 6)),
        ],
        compiler_params=pltpu.CompilerParams(
            collective_id=0, has_side_effects=True, vmem_limit_bytes=60 * 1024 * 1024
        ),
    )(query_act, key_act, value_act, short_filter, long_filter, out_weight.T, *tables)


def solution(mesh):
    placed = (
        P("ctx", "ch"),
        P("ctx", "ch"),
        P("ctx", "ch"),
        P(None, "ch"),
        P("ctx", "ch"),
        P("ch", "ctx"),
    )
    return jax.shard_map(
        local, mesh=mesh, in_specs=placed, out_specs=P("ctx", "ch"), check_vma=False
    )
```
